32 devices in a mesh: grp: 2 (over x), tile: 8 (over z, y), tok: 2 (over core).
Axes of the slice: x: 2, y: 2, z: 4, core: 2. Of those that a mesh axis runs over, the one named last changes fastest.
Arguments:
- resid: bfloat16 [3584, 8192], P(('grp', 'tok'), 'tile'), parts along dimension 0, may hold values from -17 to 17, as said below
- labels: int32 [3584], P('grp'), parts along dimension 0, may hold values from 0 to 2047
- owner: int32 [216], replicated, may hold values from 0 to 215, each once
Outputs:
- cov_tiles: float32 [432, 512, 512], P(('grp', 'tile'), 'tok'), parts along dimension 0
The draws below stay inside these ranges and needn't reach their ends.
There are 2 independent parts, one for each index of `grp`. The reference program is written for one: setup_inputs(seed, part) draws one part's arguments, and reference() takes and returns one part's arrays. A program takes and returns all parts, laid end to end along the dimension named above; an argument that names none is the same for every part. Nothing has to cross between parts.
Inputs may be any that keep to these rules, and one draw needn't show every extreme that they name: resid has per-column offsets and scales. owner is a permutation; owner[t] for t < 210 is the slot of task t, and the other entries name empty slots.
All inputs are finite; a program needn't handle non-finite values.
Results may differ from the reference program's by a relative error of at most 0.0003.
Values may be sent and summed in bfloat16 or wider, within the bound.
A program may use at most 192 MiB of HBM per device.

```python
import math
import jax
import jax.numpy as jnp
import numpy as np
from jax import lax

D = 8192
C = 2048
TILE = 512
TOKENS = 1792
PANELS = 20
TASKS = 210
SLOTS = 216


def draw_resid(key, part):
    key = jax.random.fold_in(key, 11)
    key_scale, key_centre, key_noise = jax.random.split(key, 3)
    scale = jnp.exp(jax.random.uniform(key_scale, (D,), jnp.float32, -1.2, 1.2))
    centre = jax.random.uniform(key_centre, (D,), jnp.float32, -1.0, 1.0)
    noise = jnp.clip(jax.random.normal(key_noise, (TOKENS, D), jnp.float32), -4.0, 4.0)
    return ((centre[None, :] + noise) * scale[None, :]).astype(jnp.bfloat16)


def place_ends(drawn, key, smallest, top_value):
    spot = [jax.random.randint(jax.random.fold_in(key, axis), (), 0, length) for axis, length in enumerate(drawn.shape)]
    longest = drawn.shape.index(max(drawn.shape))
    next_to = spot[:longest] + [(spot[longest] + 1) % drawn.shape[longest]] + spot[longest + 1:]
    return drawn.at[tuple(spot)].set(smallest).at[tuple(next_to)].set(top_value)


def rank_bounds(amount, slope):
    portions = [(1 << 20) // math.isqrt(standing ** slope) + 1 for standing in range(1, amount + 1)]
    width = 1 + sum(portions) // (1 << 30)
    return np.cumsum(np.array([max(1, weight // width) for weight in portions]))


def ranked_ids(key, dims, amount, slope):
    listing = rank_bounds(amount, slope)
    lot = jax.random.randint(jax.random.fold_in(key, 1), dims, 0, int(listing[amount - 1]))
    standing = jnp.searchsorted(jnp.asarray(listing, jnp.int32), lot, side="right")
    return jax.random.permutation(jax.random.fold_in(key, 2), amount)[standing].astype(jnp.int32)


def setup_inputs(seed: int = 0, part: int = 0) -> dict:
    key_list = jax.random.split(jax.random.key(seed), 4)
    own_keys = jax.random.split(jax.random.fold_in(key_list[3], part), 4)
    resid = draw_resid(jax.random.fold_in(jax.random.fold_in(key_list[3], part), 71), part)
    labels = place_ends(ranked_ids(own_keys[1], (TOKENS,), C, 2), jax.random.fold_in(own_keys[1], 3), 0, C - 1).astype(jnp.int32)
    owner = jax.random.permutation(key_list[2], SLOTS).astype(jnp.int32)
    return dict(resid=resid, labels=labels, owner=owner)


def pair_table(count):
    firsts, seconds = np.triu_indices(count)
    return np.stack([firsts, seconds], 1).astype(np.int32)


def reference(resid, labels, owner):
    total_rows = resid.shape[0]
    onehot = (labels[:, None] == jnp.arange(C, dtype=jnp.int32)[None, :]).astype(jnp.bfloat16)
    joined = jnp.concatenate([resid, onehot], 1)
    means = jnp.sum(joined, 0, dtype=jnp.float32) / total_rows
    pairs = jnp.asarray(pair_table(PANELS))

    def one(pair):
        left = lax.dynamic_slice_in_dim(joined, pair[0] * TILE, TILE, 1)
        right = lax.dynamic_slice_in_dim(joined, pair[1] * TILE, TILE, 1)
        gram = lax.dot_general(left, right, (((0,), (0,)), ((), ())), preferred_element_type=jnp.float32)
        left_mean = lax.dynamic_slice_in_dim(means, pair[0] * TILE, TILE)
        right_mean = lax.dynamic_slice_in_dim(means, pair[1] * TILE, TILE)
        return gram / total_rows - left_mean[:, None] * right_mean[None, :]

    tiles = lax.map(one, pairs)
    result = jnp.zeros((SLOTS, TILE, TILE), jnp.float32)
    return result.at[owner[:TASKS]].set(tiles)
```

```python
import functools

import jax
import jax.numpy as jnp
import numpy as np
from jax import lax
from jax.experimental import pallas as pl
from jax.experimental.pallas import tpu as pltpu
from jax.sharding import PartitionSpec as P

C = 2048
TILE = 512
PANELS = 20
TASKS = 210
BLK = 256
CHUNK = 128
MESH = pl.DeviceIdType.MESH


def pair_table(count):
    firsts, seconds = np.triu_indices(count)
    return np.stack([firsts, seconds], 1).astype(np.int32)


def kernel(cfg, idx_ref, lab_ref, x_ref, out_ref, *scratch):
    n, Z, Y, npd, own, total_rows = cfg
    g = scratch[:n]
    acc, sums, lsem, osem, rsem, ssem, xs, xr = scratch[n:]
    resid_blocks = Z * Y * npd
    label_blocks = C // BLK
    t = lax.axis_index("tile")
    k = lax.axis_index("tok")
    z, y = t // Y, t % Y
    oy = Y - 1 - y
    has_r, has_l = z < Z - 1, z > 0
    mine = pl.ds(pl.multiple_of(k * CHUNK, CHUNK), CHUNK)
    other = pl.ds(pl.multiple_of((1 - k) * CHUNK, CHUNK), CHUNK)
    right, left, peer = {"tile": t + Y}, {"tile": t - Y}, {"tile": z * Y + oy}
    sib = {"tok": 1 - k}

    def two_way(c):
        return Y > 1 and c > 0

    def cell(c, zz, yy):
        return g[c].at[pl.ds((yy * Z + zz) * npd, npd), mine, :]

    def remote(way, c, zz, yy):
        part = cell(c, zz, yy)
        return pltpu.make_async_remote_copy(
            src_ref=part,
            dst_ref=part,
            send_sem=ssem.at[way, c, yy * Z + zz],
            recv_sem=rsem.at[c, yy * Z + zz],
            device_id=(right, left, peer)[way],
            device_id_type=MESH,
        )

    def across(c, yy, half):
        part = g[c].at[pl.ds(yy * Z * npd, Z * npd), half, :]
        return pltpu.make_async_remote_copy(
            src_ref=part,
            dst_ref=part,
            send_sem=xs.at[c, yy],
            recv_sem=xr.at[c, yy],
            device_id=sib,
            device_id_type=MESH,
        )

    for c in range(n):
        for j in range(npd):
            pltpu.make_async_copy(
                x_ref.at[pl.ds(c * CHUNK, CHUNK), pl.ds(j * BLK, BLK)],
                g[c].at[(y * Z + z) * npd + j, mine, :],
                lsem.at[c],
            ).start()

    barrier = pltpu.get_barrier_semaphore()

    @pl.when(has_r)
    def _():
        pl.semaphore_signal(barrier, inc=1, device_id=right, device_id_type=MESH)

    @pl.when(has_l)
    def _():
        pl.semaphore_signal(barrier, inc=1, device_id=left, device_id_type=MESH)

    if Y > 1:
        pl.semaphore_signal(barrier, inc=1, device_id=peer, device_id_type=MESH)
    pl.semaphore_signal(barrier, inc=1, device_id=sib, device_id_type=MESH)
    near = 1 + (Y > 1)
    pl.semaphore_wait(barrier, near + jnp.where(has_r, 1, 0) + jnp.where(has_l, 1, 0))

    def push(c, zz, yy):
        @pl.when(has_r)
        def _():
            remote(0, c, zz, yy).start()

        @pl.when(has_l)
        def _():
            remote(1, c, zz, yy).start()

    def own_here(c):
        pltpu.make_async_copy(cell(c, z, y), cell(c, z, y), lsem.at[c]).wait()

    def along(c, j, yy):
        @pl.when(z - j >= 0)
        def _():
            remote(0, c, z - j, yy).wait_recv()

            @pl.when(has_r)
            def _():
                remote(0, c, z - j, yy).start()

            if two_way(c):
                remote(2, c, z - j, yy).start()

        @pl.when(z + j < Z)
        def _():
            remote(1, c, z + j, yy).wait_recv()

            @pl.when(has_l)
            def _():
                remote(1, c, z + j, yy).start()

            if two_way(c):
                remote(2, c, z + j, yy).start()

    def from_peer(c, j):
        @pl.when(z - j >= 0)
        def _():
            remote(2, c, z - j, oy).wait_recv()

        @pl.when(z + j < Z)
        def _():
            remote(2, c, z + j, oy).wait_recv()

    def wait_sent(c):
        rows = [y] if two_way(c) or Y == 1 else [y, oy]

        def one(zz, _):
            for yy in rows:
                @pl.when(has_r & (zz <= z))
                def _():
                    remote(0, c, zz, yy).wait_send()

                @pl.when(has_l & (zz >= z))
                def _():
                    remote(1, c, zz, yy).wait_send()

            if two_way(c):
                remote(2, c, zz, y).wait_send()
            return 0

        lax.fori_loop(0, Z, one, 0)
        if Y > 1 and not two_way(c):
            remote(2, c, z, y).wait_send()
        for yy in range(Y):
            across(c, yy, mine).wait_send()

    def label_rows(c):
        marks = lab_ref[c]
        lanes = lax.broadcasted_iota(jnp.int32, (2 * CHUNK, BLK), 1)
        for h in range(label_blocks):
            hit = marks == lanes + h * BLK
            g[c][resid_blocks + h] = jnp.where(hit, 1.0, 0.0).astype(jnp.bfloat16)

    def column_sums(c):
        def one(b, _):
            part = jnp.sum(g[c][b].astype(jnp.float32), 0, keepdims=True)
            sums[b] = part if c == 0 else sums[b] + part
            return 0

        lax.fori_loop(0, resid_blocks + label_blocks, one, 0)

    def product(c, i):
        lhs = g[c][idx_ref[i, 0]]
        parts = []
        for h in range(TILE // BLK):
            rhs = g[c][idx_ref[i, 1 + h]]
            parts.append(
                lax.dot_general(
                    lhs, rhs, (((0,), (0,)), ((), ())), preferred_element_type=jnp.float32
                )
            )
        return parts

    def add_tiles(c, lo, hi):
        def one(i, _):
            for h, part in enumerate(product(c, i)):
                cols = slice(h * BLK, (h + 1) * BLK)
                acc[i, :, cols] = part if c == 0 else acc[i, :, cols] + part
            return 0

        lax.fori_loop(lo, hi, one, 0)

    def finish(c):
        def one(i, _):
            keep = idx_ref[i, 3] > 0
            row = jnp.broadcast_to(sums[idx_ref[i, 0]] / total_rows, (8, BLK))
            col = jnp.transpose(row)[:, :1]
            for h, part in enumerate(product(c, i)):
                cols = slice(h * BLK, (h + 1) * BLK)
                mean = sums[idx_ref[i, 1 + h]] / total_rows
                value = (acc[i, :, cols] + part) / total_rows - col * mean
                acc[i, :, cols] = jnp.where(keep, value, 0.0)
            pltpu.make_async_copy(acc.at[i], out_ref.at[i], osem).start()
            return 0

        lax.fori_loop(0, own, one, 0)

    own_here(0)
    push(0, z, y)
    if Y > 1:
        remote(2, 0, z, y).start()
    for c in range(1, n):
        own_here(c)
        if c == 1:
            push(1, z, y)
        if Y > 1:
            remote(2, c, z, y).start()

    for ph in range(n + 1):
        if ph > 0 and ph + 1 < n:
            push(ph + 1, z, y)
        if ph < n:
            label_rows(ph)
            if Y > 1 and not two_way(ph):
                remote(2, ph, z, oy).wait_recv()
                push(ph, z, oy)
        done = ph - 2
        if done >= 0:
            for yy in range(Y):
                across(done, yy, other).wait_recv()
            column_sums(done)
        if 1 <= ph and two_way(ph - 1):
            remote(2, ph - 1, z, oy).wait_recv()

        def step(j, _):
            if ph < n:
                along(ph, j, y)
                if Y > 1 and not two_way(ph):
                    along(ph, j, oy)
            if ph >= 1 and two_way(ph - 1):
                from_peer(ph - 1, j)
            if done >= 0:
                add_tiles(done, (j - 1) * own // (Z - 1), j * own // (Z - 1))
            return 0

        lax.fori_loop(1, Z, step, 0)
        if ph < n:
            across(ph, y, mine).start()
            if Y > 1 and not two_way(ph):
                across(ph, oy, mine).start()
        if ph >= 1 and two_way(ph - 1):
            across(ph - 1, oy, mine).start()
        if done >= 0:
            wait_sent(done)

    for yy in range(Y):
        across(n - 1, yy, other).wait_recv()
    column_sums(n - 1)
    finish(n - 1)
    wait_sent(n - 1)
    pltpu.make_async_copy(acc, out_ref, osem).wait()


def body(cfg, resid, labels, owner):
    n, Z, Y, npd, own, total_rows = cfg
    place = lax.axis_index("tile")
    half = lax.axis_index("tok")
    inverse = (
        jnp.full(owner.shape, TASKS, jnp.int32)
        .at[owner[:TASKS]]
        .set(jnp.arange(TASKS, dtype=jnp.int32))
    )
    tasks = lax.dynamic_slice_in_dim(inverse, place * own, own)

    resid_blocks = Z * Y * npd
    spot = np.arange(PANELS * TILE // BLK)
    source = spot // npd
    held = ((source % Y) * Z + source // Y) * npd + spot % npd
    spot = np.where(spot < resid_blocks, held, spot).astype(np.int32)
    pairs = pair_table(PANELS)
    firsts, seconds = pairs[:, 0], pairs[:, 1]
    table = np.stack(
        [spot[2 * firsts], spot[2 * firsts + 1], spot[2 * seconds], spot[2 * seconds + 1],
         np.ones(TASKS, np.int32)], 1)
    table = jnp.asarray(np.concatenate([table, np.zeros((1, 5), np.int32)], 0))
    rows = table[tasks]
    lead = jnp.where(half == 0, rows[:, 0], rows[:, 1])
    idx = jnp.stack([lead, rows[:, 2], rows[:, 3], rows[:, 4]], 1)
    marks = labels.reshape(2, n, CHUNK).transpose(1, 0, 2).reshape(n, 2 * CHUNK, 1)

    blocks = PANELS * TILE // BLK
    flops = 2 * own * TILE // 2 * TILE * total_rows
    return pl.pallas_call(
        functools.partial(kernel, cfg),
        out_shape=jax.ShapeDtypeStruct((own, BLK, TILE), jnp.float32),
        in_specs=[
            pl.BlockSpec(memory_space=pltpu.SMEM),
            pl.BlockSpec(memory_space=pltpu.VMEM),
            pl.BlockSpec(memory_space=pl.ANY),
        ],
        out_specs=pl.BlockSpec(memory_space=pl.ANY),
        scratch_shapes=[pltpu.VMEM((blocks, 2 * CHUNK, BLK), jnp.bfloat16) for _ in range(n)]
        + [
            pltpu.VMEM((own, BLK, TILE), jnp.float32),
            pltpu.VMEM((blocks, 1, BLK), jnp.float32),
            pltpu.SemaphoreType.DMA((n,)),
            pltpu.SemaphoreType.DMA,
            pltpu.SemaphoreType.DMA((n, Z * Y)),
            pltpu.SemaphoreType.DMA((3, n, Z * Y)),
            pltpu.SemaphoreType.DMA((n, Y)),
            pltpu.SemaphoreType.DMA((n, Y)),
        ],
        compiler_params=pltpu.CompilerParams(
            collective_id=0, has_side_effects=True, vmem_limit_bytes=60 * 1024 * 1024
        ),
        cost_estimate=pl.CostEstimate(
            flops=flops, bytes_accessed=own * BLK * TILE * 4, transcendentals=0
        ),
    )(idx, marks, resid)


def solution(mesh):
    tiles = mesh.shape["tile"]

    def whole(resid, labels, owner):
        here = resid.shape[0] // mesh.shape["grp"] // mesh.shape["tok"]
        Y = 2 if tiles <= 8 else 1
        cfg = (
            here // CHUNK,
            tiles // Y,
            Y,
            resid.shape[1] // tiles // BLK,
            owner.shape[0] // tiles,
            labels.shape[0] // mesh.shape["grp"],
        )
        return jax.shard_map(
            functools.partial(body, cfg),
            mesh=mesh,
            in_specs=(P(("grp", "tok"), "tile"), P("grp"), P()),
            out_specs=P(("grp", "tile"), "tok", None),
            check_vma=False,
        )(resid, labels, owner)

    return whole
```

```python
import functools

import jax
import jax.numpy as jnp
import numpy as np
from jax import lax
from jax.experimental import pallas as pl
from jax.experimental.pallas import tpu as pltpu
from jax.sharding import PartitionSpec as P

C = 2048
TILE = 512
PANELS = 20
TASKS = 210
BLK = 256
CHUNK = 128
MESH = pl.DeviceIdType.MESH


def pair_table(count):
    firsts, seconds = np.triu_indices(count)
    return np.stack([firsts, seconds], 1).astype(np.int32)


def products(blocks, idx_ref, i):
    lhs = blocks[idx_ref[i, 0]]
    parts = []
    for h in range(TILE // BLK):
        rhs = blocks[idx_ref[i, 1 + h]]
        parts.append(
            lax.dot_general(
                lhs, rhs, (((0,), (0,)), ((), ())), preferred_element_type=jnp.float32
            )
        )
    return parts


def finish(total_rows, idx_ref, sums, acc, out_ref, tiles, sem):
    scale = 1.0 / total_rows

    def one(i, _):
        keep = jnp.where(idx_ref[i, 3] > 0, scale, 0.0)
        row = jnp.broadcast_to(sums[idx_ref[i, 0]] * scale, (8, BLK))
        col = jnp.transpose(row)[:, :1]
        for h in range(TILE // BLK):
            cols = slice(h * BLK, (h + 1) * BLK)
            tiles[i, :, cols] = (acc[i, :, cols] - col * sums[idx_ref[i, 1 + h]]) * keep
        pltpu.make_async_copy(tiles.at[i], out_ref.at[i], sem).start()
        return 0

    lax.fori_loop(0, tiles.shape[0], one, 0)
    pltpu.make_async_copy(tiles, out_ref, sem).wait()


def kernel(cfg, idx_ref, lab_ref, x_ref, acc, sums, *scratch):
    n, Z, Y, npd, own, total_rows = cfg
    g = scratch[:n]
    lsem, rsem, ssem, xs, xr = scratch[n:]
    resid_blocks = Z * Y * npd
    label_blocks = C // BLK
    t = lax.axis_index("tile")
    k = lax.axis_index("tok")
    z, y = t // Y, t % Y
    oy = Y - 1 - y
    has_r, has_l = z < Z - 1, z > 0
    mine = pl.ds(pl.multiple_of(k * CHUNK, CHUNK), CHUNK)
    other = pl.ds(pl.multiple_of((1 - k) * CHUNK, CHUNK), CHUNK)
    right, left, peer = {"tile": t + Y}, {"tile": t - Y}, {"tile": z * Y + oy}
    sib = {"tok": 1 - k}

    def two_way(c):
        return Y > 1 and c > 0

    def cell(c, zz, yy):
        return g[c].at[pl.ds((yy * Z + zz) * npd, npd), mine, :]

    def remote(way, c, zz, yy):
        part = cell(c, zz, yy)
        return pltpu.make_async_remote_copy(
            src_ref=part,
            dst_ref=part,
            send_sem=ssem.at[way, c, yy * Z + zz],
            recv_sem=rsem.at[c, yy * Z + zz],
            device_id=(right, left, peer)[way],
            device_id_type=MESH,
        )

    def across(c, yy, half):
        part = g[c].at[pl.ds(yy * Z * npd, Z * npd), half, :]
        return pltpu.make_async_remote_copy(
            src_ref=part,
            dst_ref=part,
            send_sem=xs.at[c, yy],
            recv_sem=xr.at[c, yy],
            device_id=sib,
            device_id_type=MESH,
        )

    for c in range(n):
        for j in range(npd):
            pltpu.make_async_copy(
                x_ref.at[pl.ds(c * CHUNK, CHUNK), pl.ds(j * BLK, BLK)],
                g[c].at[(y * Z + z) * npd + j, mine, :],
                lsem.at[c],
            ).start()

    barrier = pltpu.get_barrier_semaphore()

    @pl.when(has_r)
    def _():
        pl.semaphore_signal(barrier, inc=1, device_id=right, device_id_type=MESH)

    @pl.when(has_l)
    def _():
        pl.semaphore_signal(barrier, inc=1, device_id=left, device_id_type=MESH)

    if Y > 1:
        pl.semaphore_signal(barrier, inc=1, device_id=peer, device_id_type=MESH)
    pl.semaphore_signal(barrier, inc=1, device_id=sib, device_id_type=MESH)
    near = 1 + (Y > 1)
    pl.semaphore_wait(barrier, near + jnp.where(has_r, 1, 0) + jnp.where(has_l, 1, 0))

    def push(c, zz, yy):
        @pl.when(has_r)
        def _():
            remote(0, c, zz, yy).start()

        @pl.when(has_l)
        def _():
            remote(1, c, zz, yy).start()

    def own_here(c):
        pltpu.make_async_copy(cell(c, z, y), cell(c, z, y), lsem.at[c]).wait()

    def along(c, j, yy):
        @pl.when(z - j >= 0)
        def _():
            remote(0, c, z - j, yy).wait_recv()

            @pl.when(has_r)
            def _():
                remote(0, c, z - j, yy).start()

            if two_way(c):
                remote(2, c, z - j, yy).start()

        @pl.when(z + j < Z)
        def _():
            remote(1, c, z + j, yy).wait_recv()

            @pl.when(has_l)
            def _():
                remote(1, c, z + j, yy).start()

            if two_way(c):
                remote(2, c, z + j, yy).start()

    def from_peer(c, j):
        @pl.when(z - j >= 0)
        def _():
            remote(2, c, z - j, oy).wait_recv()

        @pl.when(z + j < Z)
        def _():
            remote(2, c, z + j, oy).wait_recv()

    def wait_sent(c):
        rows = [y] if two_way(c) or Y == 1 else [y, oy]

        def one(zz, _):
            for yy in rows:
                @pl.when(has_r & (zz <= z))
                def _():
                    remote(0, c, zz, yy).wait_send()

                @pl.when(has_l & (zz >= z))
                def _():
                    remote(1, c, zz, yy).wait_send()

            if two_way(c):
                remote(2, c, zz, y).wait_send()
            return 0

        lax.fori_loop(0, Z, one, 0)
        if Y > 1 and not two_way(c):
            remote(2, c, z, y).wait_send()
        for yy in range(Y):
            across(c, yy, mine).wait_send()

    def label_rows(c):
        marks = lab_ref[c]
        lanes = lax.broadcasted_iota(jnp.int32, (2 * CHUNK, BLK), 1)
        for h in range(label_blocks):
            hit = marks == lanes + h * BLK
            g[c][resid_blocks + h] = jnp.where(hit, 1.0, 0.0).astype(jnp.bfloat16)

    def column_sums(c, first, count):
        def one(b, _):
            part = jnp.sum(g[c][b].astype(jnp.float32), 0, keepdims=True)
            sums[b] = part if c == 0 else sums[b] + part
            return 0

        lax.fori_loop(first, first + count, one, 0)

    def add_tiles(c, lo, hi):
        def one(i, _):
            for h, part in enumerate(products(g[c], idx_ref, i)):
                cols = slice(h * BLK, (h + 1) * BLK)
                acc[i, :, cols] = part if c == 0 else acc[i, :, cols] + part
            return 0

        lax.fori_loop(lo, hi, one, 0)

    own_here(0)
    push(0, z, y)
    if Y > 1:
        remote(2, 0, z, y).start()
    for c in range(1, n):
        own_here(c)
        if c == 1:
            push(1, z, y)
        if Y > 1:
            remote(2, c, z, y).start()

    for ph in range(n + 1):
        if ph > 0 and ph + 1 < n:
            push(ph + 1, z, y)
        if ph < n:
            label_rows(ph)
            if Y > 1 and not two_way(ph):
                remote(2, ph, z, oy).wait_recv()
                push(ph, z, oy)
        done = ph - 2
        if done >= 0:
            for yy in range(Y):
                across(done, yy, other).wait_recv()
            column_sums(done, 0, resid_blocks + label_blocks)
        if 1 <= ph and two_way(ph - 1):
            remote(2, ph - 1, z, oy).wait_recv()

        def step(j, _):
            if ph < n:
                along(ph, j, y)
                if Y > 1 and not two_way(ph):
                    along(ph, j, oy)
            if ph >= 1 and two_way(ph - 1):
                from_peer(ph - 1, j)
            if done >= 0:
                add_tiles(done, (j - 1) * own // (Z - 1), j * own // (Z - 1))
            return 0

        lax.fori_loop(1, Z, step, 0)
        if ph < n:
            across(ph, y, mine).start()
            if Y > 1 and not two_way(ph):
                across(ph, oy, mine).start()
        if ph >= 1 and two_way(ph - 1):
            across(ph - 1, oy, mine).start()
        if done >= 0:
            wait_sent(done)

    row_blocks = Z * npd
    across(n - 1, y, other).wait_recv()
    column_sums(n - 1, y * row_blocks, row_blocks)
    column_sums(n - 1, resid_blocks, label_blocks)
    if Y > 1:
        across(n - 1, oy, other).wait_recv()
        column_sums(n - 1, oy * row_blocks, row_blocks)
    add_tiles(n - 1, 0, own)
    wait_sent(n - 1)


def body(cfg, resid, labels, owner):
    n, Z, Y, npd, own, total_rows = cfg
    place = lax.axis_index("tile")
    half = lax.axis_index("tok")
    inverse = (
        jnp.full(owner.shape, TASKS, jnp.int32)
        .at[owner[:TASKS]]
        .set(jnp.arange(TASKS, dtype=jnp.int32))
    )
    tasks = lax.dynamic_slice_in_dim(inverse, place * own, own)

    resid_blocks = Z * Y * npd
    spot = np.arange(PANELS * TILE // BLK)
    source = spot // npd
    held = ((source % Y) * Z + source // Y) * npd + spot % npd
    spot = np.where(spot < resid_blocks, held, spot).astype(np.int32)
    pairs = pair_table(PANELS)
    firsts, seconds = pairs[:, 0], pairs[:, 1]
    table = np.stack(
        [spot[2 * firsts], spot[2 * firsts + 1], spot[2 * seconds], spot[2 * seconds + 1],
         np.ones(TASKS, np.int32)], 1)
    table = jnp.asarray(np.concatenate([table, np.zeros((1, 5), np.int32)], 0))
    rows = table[tasks]
    lead = jnp.where(half == 0, rows[:, 0], rows[:, 1])
    idx = jnp.stack([lead, rows[:, 2], rows[:, 3], rows[:, 4]], 1)
    marks = labels.reshape(2, n, CHUNK).transpose(1, 0, 2).reshape(n, 2 * CHUNK, 1)

    blocks = PANELS * TILE // BLK
    flops = 2 * own * TILE // 2 * TILE * total_rows
    acc, sums = pl.pallas_call(
        functools.partial(kernel, cfg),
        out_shape=[
            pltpu.VMEM((own, BLK, TILE), jnp.float32),
            pltpu.VMEM((blocks, 1, BLK), jnp.float32),
        ],
        in_specs=[
            pl.BlockSpec(memory_space=pltpu.SMEM),
            pl.BlockSpec(memory_space=pltpu.VMEM),
            pl.BlockSpec(memory_space=pl.ANY),
        ],
        out_specs=[pl.BlockSpec(memory_space=pltpu.VMEM)] * 2,
        scratch_shapes=[pltpu.VMEM((blocks, 2 * CHUNK, BLK), jnp.bfloat16) for _ in range(n)]
        + [
            pltpu.SemaphoreType.DMA((n,)),
            pltpu.SemaphoreType.DMA((n, Z * Y)),
            pltpu.SemaphoreType.DMA((3, n, Z * Y)),
            pltpu.SemaphoreType.DMA((n, Y)),
            pltpu.SemaphoreType.DMA((n, Y)),
        ],
        compiler_params=pltpu.CompilerParams(
            collective_id=0, has_side_effects=True, vmem_limit_bytes=38 * 1024 * 1024
        ),
        cost_estimate=pl.CostEstimate(
            flops=flops, bytes_accessed=own * BLK * TILE * 4, transcendentals=0
        ),
    )(idx, marks, resid)
    acc, sums = (pltpu.with_memory_space_constraint(a, pltpu.VMEM) for a in (acc, sums))
    return pl.pallas_call(
        functools.partial(finish, total_rows),
        out_shape=jax.ShapeDtypeStruct((own, BLK, TILE), jnp.float32),
        in_specs=[
            pl.BlockSpec(memory_space=pltpu.SMEM),
            pl.BlockSpec(memory_space=pltpu.VMEM),
            pl.BlockSpec(memory_space=pltpu.VMEM),
        ],
        out_specs=pl.BlockSpec(memory_space=pl.ANY),
        scratch_shapes=[
            pltpu.VMEM((own, BLK, TILE), jnp.float32),
            pltpu.SemaphoreType.DMA,
        ],
        compiler_params=pltpu.CompilerParams(vmem_limit_bytes=20 * 1024 * 1024),
        cost_estimate=pl.CostEstimate(
            flops=3 * own * BLK * TILE, bytes_accessed=own * BLK * TILE * 4, transcendentals=0
        ),
    )(idx, sums, acc)


def solution(mesh):
    tiles = mesh.shape["tile"]

    def whole(resid, labels, owner):
        here = resid.shape[0] // mesh.shape["grp"] // mesh.shape["tok"]
        Y = 2 if tiles <= 8 else 1
        cfg = (
            here // CHUNK,
            tiles // Y,
            Y,
            resid.shape[1] // tiles // BLK,
            owner.shape[0] // tiles,
            labels.shape[0] // mesh.shape["grp"],
        )
        return jax.shard_map(
            functools.partial(body, cfg),
            mesh=mesh,
            in_specs=(P(("grp", "tok"), "tile"), P("grp"), P()),
            out_specs=P(("grp", "tile"), "tok", None),
            check_vma=False,
        )(resid, labels, owner)

    return whole
```

```python
import functools

import jax
import jax.numpy as jnp
import numpy as np
from jax import lax
from jax.experimental import pallas as pl
from jax.experimental.pallas import tpu as pltpu
from jax.sharding import PartitionSpec as P

C = 2048
TILE = 512
PANELS = 20
TASKS = 210
BLK = 256
CHUNK = 128
MESH = pl.DeviceIdType.MESH


def pair_table(count):
    firsts, seconds = np.triu_indices(count)
    return np.stack([firsts, seconds], 1).astype(np.int32)


def products(blocks, idx_ref, i):
    lhs = blocks[idx_ref[i, 0]]
    parts = []
    for h in range(TILE // BLK):
        rhs = blocks[idx_ref[i, 1 + h]]
        parts.append(
            lax.dot_general(
                lhs, rhs, (((0,), (0,)), ((), ())), preferred_element_type=jnp.float32
            )
        )
    return parts


def finish(total_rows, idx_ref, sums, acc, last, out_ref, tiles, sem):
    scale = 1.0 / total_rows

    def one(i, _):
        keep = jnp.where(idx_ref[i, 3] > 0, scale, 0.0)
        row = jnp.broadcast_to(sums[idx_ref[i, 0]] * scale, (8, BLK))
        col = jnp.transpose(row)[:, :1]
        for h, part in enumerate(products(last, idx_ref, i)):
            cols = slice(h * BLK, (h + 1) * BLK)
            gram = acc[i, :, cols] + part
            tiles[i, :, cols] = (gram - col * sums[idx_ref[i, 1 + h]]) * keep
        pltpu.make_async_copy(tiles.at[i], out_ref.at[i], sem).start()
        return 0

    lax.fori_loop(0, tiles.shape[0], one, 0)
    pltpu.make_async_copy(tiles, out_ref, sem).wait()


def kernel(cfg, idx_ref, lab_ref, x_ref, acc, sums, last, *scratch):
    n, Z, Y, npd, own, total_rows = cfg
    g = scratch[: n - 1] + (last,)
    lsem, rsem, ssem, xs, xr = scratch[n - 1 :]
    resid_blocks = Z * Y * npd
    label_blocks = C // BLK
    t = lax.axis_index("tile")
    k = lax.axis_index("tok")
    z, y = t // Y, t % Y
    oy = Y - 1 - y
    has_r, has_l = z < Z - 1, z > 0
    mine = pl.ds(pl.multiple_of(k * CHUNK, CHUNK), CHUNK)
    other = pl.ds(pl.multiple_of((1 - k) * CHUNK, CHUNK), CHUNK)
    right, left, peer = {"tile": t + Y}, {"tile": t - Y}, {"tile": z * Y + oy}
    sib = {"tok": 1 - k}

    def two_way(c):
        return Y > 1 and c > 0

    def cell(c, zz, yy):
        return g[c].at[pl.ds((yy * Z + zz) * npd, npd), mine, :]

    def remote(way, c, zz, yy):
        part = cell(c, zz, yy)
        return pltpu.make_async_remote_copy(
            src_ref=part,
            dst_ref=part,
            send_sem=ssem.at[way, c, yy * Z + zz],
            recv_sem=rsem.at[c, yy * Z + zz],
            device_id=(right, left, peer)[way],
            device_id_type=MESH,
        )

    def across(c, yy, half):
        part = g[c].at[pl.ds(yy * Z * npd, Z * npd), half, :]
        return pltpu.make_async_remote_copy(
            src_ref=part,
            dst_ref=part,
            send_sem=xs.at[c, yy],
            recv_sem=xr.at[c, yy],
            device_id=sib,
            device_id_type=MESH,
        )

    for c in range(n):
        for j in range(npd):
            pltpu.make_async_copy(
                x_ref.at[pl.ds(c * CHUNK, CHUNK), pl.ds(j * BLK, BLK)],
                g[c].at[(y * Z + z) * npd + j, mine, :],
                lsem.at[c],
            ).start()

    barrier = pltpu.get_barrier_semaphore()

    @pl.when(has_r)
    def _():
        pl.semaphore_signal(barrier, inc=1, device_id=right, device_id_type=MESH)

    @pl.when(has_l)
    def _():
        pl.semaphore_signal(barrier, inc=1, device_id=left, device_id_type=MESH)

    if Y > 1:
        pl.semaphore_signal(barrier, inc=1, device_id=peer, device_id_type=MESH)
    pl.semaphore_signal(barrier, inc=1, device_id=sib, device_id_type=MESH)
    near = 1 + (Y > 1)
    pl.semaphore_wait(barrier, near + jnp.where(has_r, 1, 0) + jnp.where(has_l, 1, 0))

    def push(c, zz, yy):
        @pl.when(has_r)
        def _():
            remote(0, c, zz, yy).start()

        @pl.when(has_l)
        def _():
            remote(1, c, zz, yy).start()

    def own_here(c):
        pltpu.make_async_copy(cell(c, z, y), cell(c, z, y), lsem.at[c]).wait()

    def along(c, j, yy):
        @pl.when(z - j >= 0)
        def _():
            remote(0, c, z - j, yy).wait_recv()

            @pl.when(has_r)
            def _():
                remote(0, c, z - j, yy).start()

            if two_way(c):
                remote(2, c, z - j, yy).start()

        @pl.when(z + j < Z)
        def _():
            remote(1, c, z + j, yy).wait_recv()

            @pl.when(has_l)
            def _():
                remote(1, c, z + j, yy).start()

            if two_way(c):
                remote(2, c, z + j, yy).start()

    def from_peer(c, j):
        @pl.when(z - j >= 0)
        def _():
            remote(2, c, z - j, oy).wait_recv()

        @pl.when(z + j < Z)
        def _():
            remote(2, c, z + j, oy).wait_recv()

    def wait_sent(c):
        rows = [y] if two_way(c) or Y == 1 else [y, oy]

        def one(zz, _):
            for yy in rows:
                @pl.when(has_r & (zz <= z))
                def _():
                    remote(0, c, zz, yy).wait_send()

                @pl.when(has_l & (zz >= z))
                def _():
                    remote(1, c, zz, yy).wait_send()

            if two_way(c):
                remote(2, c, zz, y).wait_send()
            return 0

        lax.fori_loop(0, Z, one, 0)
        if Y > 1 and not two_way(c):
            remote(2, c, z, y).wait_send()
        for yy in range(Y):
            across(c, yy, mine).wait_send()

    def label_rows(c):
        marks = lab_ref[c]
        lanes = lax.broadcasted_iota(jnp.int32, (2 * CHUNK, BLK), 1)
        for h in range(label_blocks):
            hit = marks == lanes + h * BLK
            g[c][resid_blocks + h] = jnp.where(hit, 1.0, 0.0).astype(jnp.bfloat16)

    def column_sums(c, first, count):
        def one(b, _):
            part = jnp.sum(g[c][b].astype(jnp.float32), 0, keepdims=True)
            sums[b] = part if c == 0 else sums[b] + part
            return 0

        lax.fori_loop(first, first + count, one, 0)

    def add_tiles(c, lo, hi):
        def one(i, _):
            for h, part in enumerate(products(g[c], idx_ref, i)):
                cols = slice(h * BLK, (h + 1) * BLK)
                acc[i, :, cols] = part if c == 0 else acc[i, :, cols] + part
            return 0

        lax.fori_loop(lo, hi, one, 0)

    own_here(0)
    push(0, z, y)
    if Y > 1:
        remote(2, 0, z, y).start()
    for c in range(1, n):
        own_here(c)
        if c == 1:
            push(1, z, y)
        if Y > 1:
            remote(2, c, z, y).start()

    for ph in range(n + 1):
        if ph > 0 and ph + 1 < n:
            push(ph + 1, z, y)
        if ph < n:
            label_rows(ph)
            if Y > 1 and not two_way(ph):
                remote(2, ph, z, oy).wait_recv()
                push(ph, z, oy)
        done = ph - 2
        if done >= 0:
            for yy in range(Y):
                across(done, yy, other).wait_recv()
            column_sums(done, 0, resid_blocks + label_blocks)
        if ph == n:
            across(n - 1, y, other).wait_recv()
            column_sums(n - 1, y * Z * npd, Z * npd)
            column_sums(n - 1, resid_blocks, label_blocks)
            add_tiles(done, 0, own)
        if 1 <= ph and two_way(ph - 1):
            remote(2, ph - 1, z, oy).wait_recv()

        def step(j, _):
            if ph < n:
                along(ph, j, y)
                if Y > 1 and not two_way(ph):
                    along(ph, j, oy)
            if ph >= 1 and two_way(ph - 1):
                from_peer(ph - 1, j)
            if 0 <= done and ph < n:
                add_tiles(done, (j - 1) * own // (Z - 1), j * own // (Z - 1))
            return 0

        lax.fori_loop(1, Z, step, 0)
        if ph < n:
            across(ph, y, mine).start()
            if Y > 1 and not two_way(ph):
                across(ph, oy, mine).start()
        if ph >= 1 and two_way(ph - 1):
            across(ph - 1, oy, mine).start()
        if done >= 0:
            wait_sent(done)

    if Y > 1:
        across(n - 1, oy, other).wait_recv()
        column_sums(n - 1, oy * Z * npd, Z * npd)
    wait_sent(n - 1)


def body(cfg, resid, labels, owner):
    n, Z, Y, npd, own, total_rows = cfg
    place = lax.axis_index("tile")
    half = lax.axis_index("tok")
    resid_blocks = Z * Y * npd
    spot = np.arange(PANELS * TILE // BLK)
    source = spot // npd
    held = ((source % Y) * Z + source // Y) * npd + spot % npd
    spot = np.where(spot < resid_blocks, held, spot).astype(np.int32)
    pairs = pair_table(PANELS)
    firsts, seconds = pairs[:, 0], pairs[:, 1]
    leads = jnp.where(half == 0, spot[2 * firsts], spot[2 * firsts + 1])
    columns = [leads, spot[2 * seconds], spot[2 * seconds + 1], np.ones(TASKS, np.int32)]
    table = jnp.stack([jnp.asarray(column) for column in columns])
    slots = place * own + jnp.arange(own, dtype=jnp.int32)
    found = owner[None, None, :TASKS] == slots[:, None, None]
    idx = jnp.sum(jnp.where(found, table[None], 0), 2)
    marks = labels.reshape(2, n, CHUNK).transpose(1, 0, 2).reshape(n, 2 * CHUNK, 1)

    blocks = PANELS * TILE // BLK
    flops = 2 * own * TILE // 2 * TILE * total_rows
    acc, sums, last = pl.pallas_call(
        functools.partial(kernel, cfg),
        out_shape=[
            pltpu.VMEM((own, BLK, TILE), jnp.float32),
            pltpu.VMEM((blocks, 1, BLK), jnp.float32),
            pltpu.VMEM((blocks, 2 * CHUNK, BLK), jnp.bfloat16),
        ],
        in_specs=[
            pl.BlockSpec(memory_space=pltpu.SMEM),
            pl.BlockSpec(memory_space=pltpu.VMEM),
            pl.BlockSpec(memory_space=pl.ANY),
        ],
        out_specs=[pl.BlockSpec(memory_space=pltpu.VMEM)] * 3,
        scratch_shapes=[pltpu.VMEM((blocks, 2 * CHUNK, BLK), jnp.bfloat16) for _ in range(n - 1)]
        + [
            pltpu.SemaphoreType.DMA((n,)),
            pltpu.SemaphoreType.DMA((n, Z * Y)),
            pltpu.SemaphoreType.DMA((3, n, Z * Y)),
            pltpu.SemaphoreType.DMA((n, Y)),
            pltpu.SemaphoreType.DMA((n, Y)),
        ],
        compiler_params=pltpu.CompilerParams(
            collective_id=0, has_side_effects=True, vmem_limit_bytes=32 * 1024 * 1024
        ),
        cost_estimate=pl.CostEstimate(
            flops=flops, bytes_accessed=own * BLK * TILE * 4, transcendentals=0
        ),
    )(idx, marks, resid)
    held = [pltpu.with_memory_space_constraint(a, pltpu.VMEM) for a in (sums, acc, last)]
    return pl.pallas_call(
        functools.partial(finish, total_rows),
        out_shape=jax.ShapeDtypeStruct((own, BLK, TILE), jnp.float32),
        in_specs=[
            pl.BlockSpec(memory_space=pltpu.SMEM),
            pl.BlockSpec(memory_space=pltpu.VMEM),
            pl.BlockSpec(memory_space=pltpu.VMEM),
            pl.BlockSpec(memory_space=pltpu.VMEM),
        ],
        out_specs=pl.BlockSpec(memory_space=pl.ANY),
        scratch_shapes=[
            pltpu.VMEM((own, BLK, TILE), jnp.float32),
            pltpu.SemaphoreType.DMA,
        ],
        compiler_params=pltpu.CompilerParams(vmem_limit_bytes=14 * 1024 * 1024),
        cost_estimate=pl.CostEstimate(
            flops=flops // n, bytes_accessed=own * BLK * TILE * 4, transcendentals=0
        ),
    )(idx, *held)


def solution(mesh):
    tiles = mesh.shape["tile"]

    def whole(resid, labels, owner):
        here = resid.shape[0] // mesh.shape["grp"] // mesh.shape["tok"]
        Y = 2 if tiles <= 8 else 1
        cfg = (
            here // CHUNK,
            tiles // Y,
            Y,
            resid.shape[1] // tiles // BLK,
            owner.shape[0] // tiles,
            labels.shape[0] // mesh.shape["grp"],
        )
        return jax.shard_map(
            functools.partial(body, cfg),
            mesh=mesh,
            in_specs=(P(("grp", "tok"), "tile"), P("grp"), P()),
            out_specs=P(("grp", "tile"), "tok", None),
            check_vma=False,
        )(resid, labels, owner)

    return whole
```

```python
import functools

import jax
import jax.numpy as jnp
import numpy as np
from jax import lax
from jax.experimental import pallas as pl
from jax.experimental.pallas import tpu as pltpu
from jax.sharding import PartitionSpec as P

C = 2048
TILE = 512
PANELS = 20
TASKS = 210
BLK = 256
CHUNK = 128
MESH = pl.DeviceIdType.MESH


def pair_table(count):
    firsts, seconds = np.triu_indices(count)
    return np.stack([firsts, seconds], 1).astype(np.int32)


def products(blocks, idx_ref, i):
    lhs = blocks[idx_ref[i, 0]]
    parts = []
    for h in range(TILE // BLK):
        rhs = blocks[idx_ref[i, 1 + h]]
        parts.append(
            lax.dot_general(
                lhs, rhs, (((0,), (0,)), ((), ())), preferred_element_type=jnp.float32
            )
        )
    return parts


def finish(total_rows, idx_ref, sums, acc, last, out_ref, tiles, sem):
    scale = 1.0 / total_rows

    def one(i, _):
        keep = jnp.where(idx_ref[i, 3] > 0, scale, 0.0)
        row = jnp.broadcast_to(sums[idx_ref[i, 0]] * scale, (8, BLK))
        col = jnp.transpose(row)[:, :1]
        for h, part in enumerate(products(last, idx_ref, i)):
            cols = slice(h * BLK, (h + 1) * BLK)
            gram = acc[i, :, cols] + part
            tiles[i, :, cols] = (gram - col * sums[idx_ref[i, 1 + h]]) * keep
        pltpu.make_async_copy(tiles.at[i], out_ref.at[i], sem).start()
        return 0

    lax.fori_loop(0, tiles.shape[0], one, 0)
    pltpu.make_async_copy(tiles, out_ref, sem).wait()


def kernel(cfg, idx_ref, lab_ref, x_ref, acc, sums, last, *scratch):
    n, Z, Y, npd, own, total_rows = cfg
    g = scratch[: n - 1] + (last,)
    lsem, rsem, ssem, xs, xr = scratch[n - 1 :]
    resid_blocks = Z * Y * npd
    label_blocks = C // BLK
    t = lax.axis_index("tile")
    k = lax.axis_index("tok")
    z, y = t // Y, t % Y
    oy = Y - 1 - y
    has_r, has_l = z < Z - 1, z > 0
    mine = pl.ds(pl.multiple_of(k * CHUNK, CHUNK), CHUNK)
    other = pl.ds(pl.multiple_of((1 - k) * CHUNK, CHUNK), CHUNK)
    right, left, peer = {"tile": t + Y}, {"tile": t - Y}, {"tile": z * Y + oy}
    sib = {"tok": 1 - k}

    def two_way(c):
        return Y > 1 and c > 0

    def cell(c, zz, yy):
        return g[c].at[pl.ds((yy * Z + zz) * npd, npd), mine, :]

    def remote(way, c, zz, yy):
        part = cell(c, zz, yy)
        return pltpu.make_async_remote_copy(
            src_ref=part,
            dst_ref=part,
            send_sem=ssem.at[way, c, yy * Z + zz],
            recv_sem=rsem.at[c, yy * Z + zz],
            device_id=(right, left, peer)[way],
            device_id_type=MESH,
        )

    def across(c, yy, half):
        part = g[c].at[pl.ds(yy * Z * npd, Z * npd), half, :]
        return pltpu.make_async_remote_copy(
            src_ref=part,
            dst_ref=part,
            send_sem=xs.at[c, yy],
            recv_sem=xr.at[c, yy],
            device_id=sib,
            device_id_type=MESH,
        )

    for c in range(n):
        for j in range(npd):
            pltpu.make_async_copy(
                x_ref.at[pl.ds(c * CHUNK, CHUNK), pl.ds(j * BLK, BLK)],
                g[c].at[(y * Z + z) * npd + j, mine, :],
                lsem.at[c],
            ).start()

    barrier = pltpu.get_barrier_semaphore()

    @pl.when(has_r)
    def _():
        pl.semaphore_signal(barrier, inc=1, device_id=right, device_id_type=MESH)

    @pl.when(has_l)
    def _():
        pl.semaphore_signal(barrier, inc=1, device_id=left, device_id_type=MESH)

    if Y > 1:
        pl.semaphore_signal(barrier, inc=1, device_id=peer, device_id_type=MESH)
    pl.semaphore_signal(barrier, inc=1, device_id=sib, device_id_type=MESH)
    near = 1 + (Y > 1)
    pl.semaphore_wait(barrier, near + jnp.where(has_r, 1, 0) + jnp.where(has_l, 1, 0))

    def push(c, zz, yy):
        @pl.when(has_r)
        def _():
            remote(0, c, zz, yy).start()

        @pl.when(has_l)
        def _():
            remote(1, c, zz, yy).start()

    def own_here(c):
        pltpu.make_async_copy(cell(c, z, y), cell(c, z, y), lsem.at[c]).wait()

    def along(c, j, yy):
        @pl.when(z - j >= 0)
        def _():
            remote(0, c, z - j, yy).wait_recv()

            @pl.when(has_r)
            def _():
                remote(0, c, z - j, yy).start()

            if two_way(c):
                remote(2, c, z - j, yy).start()

        @pl.when(z + j < Z)
        def _():
            remote(1, c, z + j, yy).wait_recv()

            @pl.when(has_l)
            def _():
                remote(1, c, z + j, yy).start()

            if two_way(c):
                remote(2, c, z + j, yy).start()

    def from_peer(c, j):
        @pl.when(z - j >= 0)
        def _():
            remote(2, c, z - j, oy).wait_recv()

        @pl.when(z + j < Z)
        def _():
            remote(2, c, z + j, oy).wait_recv()

    def wait_sent(c):
        rows = [y] if two_way(c) or Y == 1 else [y, oy]

        def one(zz, _):
            for yy in rows:
                @pl.when(has_r & (zz <= z))
                def _():
                    remote(0, c, zz, yy).wait_send()

                @pl.when(has_l & (zz >= z))
                def _():
                    remote(1, c, zz, yy).wait_send()

            if two_way(c):
                remote(2, c, zz, y).wait_send()
            return 0

        lax.fori_loop(0, Z, one, 0)
        if Y > 1 and not two_way(c):
            remote(2, c, z, y).wait_send()
        for yy in range(Y):
            across(c, yy, mine).wait_send()

    def label_rows(c):
        marks = lab_ref[c]
        lanes = lax.broadcasted_iota(jnp.int32, (2 * CHUNK, BLK), 1)
        for h in range(label_blocks):
            hit = marks == lanes + h * BLK
            g[c][resid_blocks + h] = jnp.where(hit, 1.0, 0.0).astype(jnp.bfloat16)

    def column_sums(c, first, count):
        def one(b, _):
            part = jnp.sum(g[c][b].astype(jnp.float32), 0, keepdims=True)
            sums[b] = part if c == 0 else sums[b] + part
            return 0

        lax.fori_loop(first, first + count, one, 0)

    def add_tiles(c, lo, hi):
        def one(i, _):
            for h, part in enumerate(products(g[c], idx_ref, i)):
                cols = slice(h * BLK, (h + 1) * BLK)
                acc[i, :, cols] = part if c == 0 else acc[i, :, cols] + part
            return 0

        lax.fori_loop(lo, hi, one, 0)

    own_here(0)
    push(0, z, y)
    if Y > 1:
        remote(2, 0, z, y).start()
    for c in range(1, n):
        own_here(c)
        if c == 1:
            push(1, z, y)
        if Y > 1:
            remote(2, c, z, y).start()

    for ph in range(n + 1):
        if ph > 0 and ph + 1 < n:
            push(ph + 1, z, y)
        if ph < n:
            label_rows(ph)
            if Y > 1 and not two_way(ph):
                remote(2, ph, z, oy).wait_recv()
                push(ph, z, oy)
        done = ph - 2
        if done >= 0:
            for yy in range(Y):
                across(done, yy, other).wait_recv()
            if ph == n:
                column_sums(done, 0, resid_blocks + label_blocks)
        if ph == n:
            across(n - 1, y, other).wait_recv()
            column_sums(n - 1, y * Z * npd, Z * npd)
            column_sums(n - 1, resid_blocks, label_blocks)
            add_tiles(done, 0, own)
        if 1 <= ph and two_way(ph - 1):
            remote(2, ph - 1, z, oy).wait_recv()

        def step(j, _):
            if ph < n:
                along(ph, j, y)
                if Y > 1 and not two_way(ph):
                    along(ph, j, oy)
            if ph >= 1 and two_way(ph - 1):
                from_peer(ph - 1, j)
            if 0 <= done and ph < n:
                total = resid_blocks + label_blocks
                begin = (j - 1) * total // (Z - 1)
                column_sums(done, begin, j * total // (Z - 1) - begin)
                add_tiles(done, (j - 1) * own // (Z - 1), j * own // (Z - 1))
            return 0

        lax.fori_loop(1, Z, step, 0)
        if ph < n:
            across(ph, y, mine).start()
            if Y > 1 and not two_way(ph):
                across(ph, oy, mine).start()
        if ph >= 1 and two_way(ph - 1):
            across(ph - 1, oy, mine).start()
        if done >= 0:
            wait_sent(done)

    if Y > 1:
        across(n - 1, oy, other).wait_recv()
        column_sums(n - 1, oy * Z * npd, Z * npd)
    wait_sent(n - 1)


def body(cfg, resid, labels, owner):
    n, Z, Y, npd, own, total_rows = cfg
    place = lax.axis_index("tile")
    half = lax.axis_index("tok")
    resid_blocks = Z * Y * npd
    spot = np.arange(PANELS * TILE // BLK)
    source = spot // npd
    held = ((source % Y) * Z + source // Y) * npd + spot % npd
    spot = np.where(spot < resid_blocks, held, spot).astype(np.int32)
    pairs = pair_table(PANELS)
    firsts, seconds = pairs[:, 0], pairs[:, 1]
    leads = jnp.where(half == 0, spot[2 * firsts], spot[2 * firsts + 1])
    columns = [leads, spot[2 * seconds], spot[2 * seconds + 1], np.ones(TASKS, np.int32)]
    table = jnp.stack([jnp.asarray(column) for column in columns])
    slots = place * own + jnp.arange(own, dtype=jnp.int32)
    found = owner[None, None, :TASKS] == slots[:, None, None]
    idx = jnp.sum(jnp.where(found, table[None], 0), 2)
    marks = labels.reshape(2, n, CHUNK).transpose(1, 0, 2).reshape(n, 2 * CHUNK, 1)

    blocks = PANELS * TILE // BLK
    flops = 2 * own * TILE // 2 * TILE * total_rows
    resid = pltpu.with_memory_space_constraint(resid, pltpu.HBM)
    acc, sums, last = pl.pallas_call(
        functools.partial(kernel, cfg),
        out_shape=[
            pltpu.VMEM((own, BLK, TILE), jnp.float32),
            pltpu.VMEM((blocks, 1, BLK), jnp.float32),
            pltpu.VMEM((blocks, 2 * CHUNK, BLK), jnp.bfloat16),
        ],
        in_specs=[
            pl.BlockSpec(memory_space=pltpu.SMEM),
            pl.BlockSpec(memory_space=pltpu.VMEM),
            pl.BlockSpec(memory_space=pl.ANY),
        ],
        out_specs=[pl.BlockSpec(memory_space=pltpu.VMEM)] * 3,
        scratch_shapes=[pltpu.VMEM((blocks, 2 * CHUNK, BLK), jnp.bfloat16) for _ in range(n - 1)]
        + [
            pltpu.SemaphoreType.DMA((n,)),
            pltpu.SemaphoreType.DMA((n, Z * Y)),
            pltpu.SemaphoreType.DMA((3, n, Z * Y)),
            pltpu.SemaphoreType.DMA((n, Y)),
            pltpu.SemaphoreType.DMA((n, Y)),
        ],
        compiler_params=pltpu.CompilerParams(
            collective_id=0, has_side_effects=True, vmem_limit_bytes=32 * 1024 * 1024
        ),
        cost_estimate=pl.CostEstimate(
            flops=flops, bytes_accessed=own * BLK * TILE * 4, transcendentals=0
        ),
    )(idx, marks, resid)
    held = [pltpu.with_memory_space_constraint(a, pltpu.VMEM) for a in (sums, acc, last)]
    return pl.pallas_call(
        functools.partial(finish, total_rows),
        out_shape=jax.ShapeDtypeStruct((own, BLK, TILE), jnp.float32),
        in_specs=[
            pl.BlockSpec(memory_space=pltpu.SMEM),
            pl.BlockSpec(memory_space=pltpu.VMEM),
            pl.BlockSpec(memory_space=pltpu.VMEM),
            pl.BlockSpec(memory_space=pltpu.VMEM),
        ],
        out_specs=pl.BlockSpec(memory_space=pl.ANY),
        scratch_shapes=[
            pltpu.VMEM((own, BLK, TILE), jnp.float32),
            pltpu.SemaphoreType.DMA,
        ],
        compiler_params=pltpu.CompilerParams(vmem_limit_bytes=14 * 1024 * 1024),
        cost_estimate=pl.CostEstimate(
            flops=flops // n, bytes_accessed=own * BLK * TILE * 4, transcendentals=0
        ),
    )(idx, *held)


def solution(mesh):
    tiles = mesh.shape["tile"]

    def whole(resid, labels, owner):
        here = resid.shape[0] // mesh.shape["grp"] // mesh.shape["tok"]
        Y = 2 if tiles <= 8 else 1
        cfg = (
            here // CHUNK,
            tiles // Y,
            Y,
            resid.shape[1] // tiles // BLK,
            owner.shape[0] // tiles,
            labels.shape[0] // mesh.shape["grp"],
        )
        return jax.shard_map(
            functools.partial(body, cfg),
            mesh=mesh,
            in_specs=(P(("grp", "tok"), "tile"), P("grp"), P()),
            out_specs=P(("grp", "tile"), "tok", None),
            check_vma=False,
        )(resid, labels, owner)

    return whole
```
